128 devices in a mesh: grp: 2 (over core), dev: 64 (over y, z, x).
Axes of the slice: x: 4, y: 4, z: 4, core: 2. Of those that a mesh axis runs over, the one named last changes fastest.
Arguments:
- hidden: bfloat16 [4096, 4096], P(('grp', 'dev')), may hold values from -6 to 6
- norm_gain: bfloat16 [4096], replicated, may hold values from 0.5 to 2
- expert_ids: int32 [4096, 8], P(('grp', 'dev')), may hold values from 0 to 63, all different within a row; in each aligned block of 32 rows (0 to 31, 32 to 63, ...) at most 8 rows name the same one
- gate_values: float32 [4096, 8], P(('grp', 'dev')), may hold values from 0.05 to 1
- w_gate: bfloat16 [64, 4096, 1536], P('dev', None, 'grp'), may hold values from -0.09375 to 0.09375
- w_up: bfloat16 [64, 4096, 1536], P('dev', None, 'grp'), may hold values from -0.09375 to 0.09375
- w_down: bfloat16 [64, 1536, 4096], P('dev', 'grp'), may hold values from -0.15625 to 0.15625
Outputs:
- mixed_out: bfloat16 [4096, 4096], P(('grp', 'dev'))
The draws below stay inside these ranges and needn't reach their ends.
Inputs may be any that keep to these rules, and one draw needn't show every extreme that they name: `expert_ids`: each row names 8 different experts; no expert is named by more than 8 rows of one aligned block of 32 rows, and in every draw some expert is named by exactly 8 rows of some block.
All inputs are finite; a program needn't handle non-finite values.
Results may differ from the reference program's by a relative error of at most 0.0051.
Values may be sent and summed in bfloat16 or wider, within the bound.
A program may use at most 128 MiB of HBM per device.

```python
import math
import jax
import jax.numpy as jnp
import numpy as np
from jax import lax

D = 4096
FF = 1536
TOP = 8
ROWS_DEV = 32
EXPERTS = 64
TOKENS = 4096
CAP = 8


def shard_levels(stream_key, extent, cuts, least, largest):
    loudness = 1.0
    for dim, parts in cuts:
        draws = jax.random.uniform(jax.random.fold_in(jax.random.fold_in(stream_key, 6), dim), (parts,), jnp.float32, least / len(cuts), largest / len(cuts))
        loudness = loudness * jnp.repeat(jnp.exp(draws), extent[dim] // parts).reshape((-1,) + (1,) * (len(extent) - 1 - dim))
    return loudness


def routed_block(own_key, own, number, rows, count, top, bound, skew):
    order = jax.random.permutation(own_key, count)
    packed, ordinary = portions_of(count, rows * top, bound, skew, True), portions_of(count, rows * top, bound, skew, False)
    places = jnp.arange(count)

    def named(tallies, rotation):
        used = int((tallies > 0).sum())
        fixed = max(1, used // 4)
        shifted = fixed + (places - fixed + rotation * (used - fixed)) % max(1, count - fixed)
        return jnp.zeros((count,), jnp.int32).at[order[jnp.where(places < fixed, places, shifted)]].set(jnp.asarray(tallies, jnp.int32))

    tallies = jnp.where(number % 4 == 0, named(packed, number // 4), named(ordinary, number - number // 4 - 1))
    mixed = jax.random.permutation(jax.random.fold_in(own, 3), count)
    donor, receiver = mixed[0:count // 2 * 2:2], mixed[1:count // 2 * 2:2]
    room = jnp.minimum(tallies[donor] - 1, bound - tallies[receiver]) // 2
    room = jnp.where((donor == order[0]) | (receiver == order[0]) | (tallies[receiver] == 0), 0, jnp.maximum(room, 0))
    shifted = jax.random.randint(jax.random.fold_in(own, 4), (count // 2,), 0, 1 << 20) % (room + 1)
    tallies = tallies.at[donor].add(-shifted).at[receiver].add(shifted)
    members = jnp.searchsorted(jnp.cumsum(tallies), jnp.arange(rows * top), side="right").astype(jnp.int32)
    listing = members.reshape(top, rows).T
    listing = listing[jax.random.permutation(jax.random.fold_in(own, 1), rows)]
    rotation = jax.random.randint(jax.random.fold_in(own, 2), (rows, 1), 0, top)
    return jnp.take_along_axis(listing, (jnp.arange(top)[None, :] + rotation) % top, axis=1)


def portions_of(amount, total, most, slope, full):
    portions = [(1 << 20) // math.isqrt(rank ** slope) + 1 for rank in range(1, amount + 1)]
    largest = most if full else min(most, max(-(-total // amount), total * portions[0] // sum(portions)))
    least = 1 if total - largest >= amount - 1 else 0
    counts, surplus = [largest] + [least] * (amount - 1), total - largest - least * (amount - 1)
    while surplus > 0:
        candidates = [i for i in range(1, amount) if counts[i] < largest] or [i for i in range(1, amount) if counts[i] < most]
        mass, left = sum([portions[i] for i in candidates]), surplus
        for i in candidates:
            more = min(most - counts[i], max(1, left * portions[i] // mass), surplus)
            counts[i] = counts[i] + more
            surplus = surplus - more
    return np.array(counts)


def scatter_about(key, extent, spread, reach, pieces=(), kind=jnp.bfloat16):
    values = spread * jax.random.normal(key, extent, jnp.float32)
    if pieces:
        values = values * shard_levels(key, extent, pieces, -0.22, 0.18)
    return jnp.clip(values, -reach, reach).astype(kind)


def setup_inputs(seed: int = 0) -> dict:
    keys = jax.random.split(jax.random.key(seed), 8)
    hidden = scatter_about(keys[0], (TOKENS, D), 1.0, 6.0, ((0, 128),))
    norm_gain = jnp.clip(jnp.exp(jax.random.uniform(keys[1], (D,), jnp.float32, math.log(0.5), math.log(2.0))), 0.5, 2.0).astype(jnp.bfloat16)
    expert_ids_keys = jax.random.split(jax.random.fold_in(keys[2], 1), TOKENS // ROWS_DEV)
    expert_ids_turns = jax.random.permutation(jax.random.fold_in(keys[2], 3), TOKENS // ROWS_DEV)
    expert_ids = jax.vmap(lambda own, number: routed_block(jax.random.fold_in(keys[2], 2), own, number, ROWS_DEV, EXPERTS, TOP, CAP, 2))(expert_ids_keys, expert_ids_turns).reshape((TOKENS, TOP))
    gate_values = jnp.clip(jnp.exp(math.log(1.0) - 2.9957323 * jax.random.uniform(keys[3], (TOKENS, TOP), jnp.float32) ** shard_levels(keys[3], (TOKENS, TOP), ((0, 128),), -0.2, 0.2)), 0.05, 1.0)
    w_gate = scatter_about(keys[4], (EXPERTS, D, FF), D ** -0.5, 0.09375, ((0, 64), (2, 2)))
    w_up = scatter_about(keys[5], (EXPERTS, D, FF), D ** -0.5, 0.09375, ((0, 64), (2, 2)))
    w_down = scatter_about(keys[6], (EXPERTS, FF, D), FF ** -0.5, 0.15625, ((0, 64), (1, 2)))
    return dict(hidden=hidden, norm_gain=norm_gain, expert_ids=expert_ids, gate_values=gate_values, w_gate=w_gate, w_up=w_up, w_down=w_down)


epsilon = 1e-06

def reference(hidden, norm_gain, expert_ids, gate_values, w_gate, w_up, w_down):
    tokens_all = hidden.shape[0]
    blocks = tokens_all // ROWS_DEV
    per_block = ROWS_DEV * TOP
    hidden_f = hidden.astype(jnp.float32)
    factor = lax.rsqrt(lax.optimization_barrier(jnp.mean(hidden_f * hidden_f, axis=1, keepdims=True)) + epsilon)
    normed = (hidden_f * factor * norm_gain.astype(jnp.float32)[None, :]).astype(jnp.bfloat16)
    weights = gate_values / lax.optimization_barrier(jnp.sum(gate_values, axis=1, keepdims=True))
    pair_expert = expert_ids.reshape(blocks, per_block)
    onehot = (pair_expert[:, :, None] == jnp.arange(EXPERTS, dtype=jnp.int32)[None, None, :]).astype(jnp.int32)
    earlier = jnp.cumsum(onehot, axis=1) - onehot
    slot_index = lax.optimization_barrier(jnp.sum(earlier * onehot, axis=2)).astype(jnp.int32)
    flat_expert = expert_ids.reshape(-1).astype(jnp.int32)
    flat_slot = slot_index.reshape(-1)
    pair_order = jnp.arange(tokens_all * TOP, dtype=jnp.int32)
    flat_block = pair_order // per_block
    flat_token = pair_order // TOP
    position = flat_block * CAP + flat_slot
    source_row = jnp.full((EXPERTS, blocks * CAP), tokens_all, jnp.int32).at[flat_expert, position].set(flat_token)
    pair_weight = jnp.zeros((EXPERTS, blocks * CAP), jnp.float32).at[flat_expert, position].set(weights.reshape(-1))
    padded = jnp.concatenate([normed, jnp.zeros((1, D), jnp.bfloat16)], axis=0)
    half_units = FF // 2

    def one_expert(total, inputs):
        gate_w, up_w, down_w, rows_e, weight_e = inputs
        taken = jnp.take(padded, rows_e, axis=0)
        gate_h = jnp.dot(taken, gate_w, preferred_element_type=jnp.float32)
        up_h = jnp.dot(taken, up_w, preferred_element_type=jnp.float32)
        active = (jax.nn.silu(gate_h) * up_h).astype(jnp.bfloat16)
        lower = jnp.dot(active[:, :half_units], down_w[:half_units], preferred_element_type=jnp.float32).astype(jnp.bfloat16)
        upper = jnp.dot(active[:, half_units:], down_w[half_units:], preferred_element_type=jnp.float32).astype(jnp.bfloat16)
        out_e = (lower.astype(jnp.float32) + upper.astype(jnp.float32)).astype(jnp.bfloat16)
        total = total.at[rows_e].add(weight_e[:, None] * out_e.astype(jnp.float32), mode='drop')
        return (total, None)
    total, _ = lax.scan(one_expert, hidden_f, (w_gate, w_up, w_down, source_row, pair_weight))
    return total.astype(jnp.bfloat16)
```

```python
import functools

import jax
import jax.numpy as jnp
from jax import lax
from jax.experimental import pallas as pl
from jax.experimental.pallas import tpu as pltpu
from jax.sharding import PartitionSpec as P

D = 4096
HALF = 768
TOP = 8
ROWS = 32
EPS = 1e-06
MESH = pl.DeviceIdType.MESH
F32, BF16 = jnp.float32, jnp.bfloat16

ORDERS = (("y", "z", "x"), ("z", "x", "y"), ("x", "y", "z"))
STRIDE = {"y": 16, "z": 4, "x": 1}
COUNT = (6, 5, 5)
BASE = (0, 1536, 2816)
WIDTH = 256
UNITS = [(r, j) for j in range(6) for r in range(3) if j < COUNT[r]]
NU = len(UNITS)
GROUPS = []
for _i in range(3):
    for _r in range(3):
        _js = [j for j in (2 * _i, 2 * _i + 1) if j < COUNT[_r]]
        GROUPS.append((_r, BASE[_r] + _js[0] * WIDTH, len(_js) * WIDTH, [UNITS.index((_r, j)) for j in _js]))
FREED = max(i for i, grp in enumerate(GROUPS) if grp[0] == 0)
EARLY = 4


def tile_map(r):
    out = []
    for p in range(64):
        at = dict(zip(ORDERS[r], (p % 4, p // 4 % 4, p // 16)))
        out.append(at[ORDERS[0][2]] * 16 + at[ORDERS[0][1]] * 4 + at[ORDERS[0][0]])
    return out


def unit_lanes(q):
    r, j = UNITS[q]
    return pl.ds(BASE[r] + j * WIDTH, WIDTH)


def aligned(index, rows):
    return pl.ds(pl.multiple_of(index * rows, rows), rows)


def wait_bytes(view, sem):
    pltpu.make_async_copy(view, view, sem).wait()


def body(hidden, gain, ids, gates, w_gate, w_up, w_down, out, down_other,
         g1, g2, sel, xs, rb, ra, acc, act, w1, wd, m1, m2, pick, mix,
         recv1, recv2, recv3, recv_c, recv_b, recv_a, recv_m1, recv_m2,
         send1, send2, send3, send_c, send_b, send_a, send_m,
         w_local, w_recv, w_send, d_recv, d_local):
    grp = lax.axis_index("grp")
    dev = lax.axis_index("dev")
    at = {"y": dev // 16, "z": (dev // 4) % 4, "x": dev % 4}

    def peer(axis, shift):
        other = (at[axis] + shift) % 4
        return other, dev + (other - at[axis]) * STRIDE[axis]

    def send(src, dst, ssem, rsem, target):
        pltpu.make_async_remote_copy(
            src_ref=src, dst_ref=dst, send_sem=ssem, recv_sem=rsem,
            device_id=(grp, target), device_id_type=MESH,
        ).start()

    barrier = pltpu.get_barrier_semaphore()
    for axis in ("y", "z", "x"):
        for shift in (1, 2, 3):
            _, target = peer(axis, shift)
            pl.semaphore_signal(barrier, inc=1, device_id=(grp, target), device_id_type=MESH)
    pl.semaphore_signal(barrier, inc=1, device_id=(1 - grp, dev), device_id_type=MESH)

    for i, (r, k0, kw, _) in enumerate(GROUPS):
        rows = pl.ds(k0, kw)
        pltpu.make_async_copy(w_gate.at[rows], w1.at[rows, pl.ds(0, HALF)], w_local.at[i]).start()
        pltpu.make_async_copy(w_up.at[rows], w1.at[rows, pl.ds(2 * HALF, HALF)], w_local.at[i]).start()
    for q in range(EARLY):
        pltpu.make_async_copy(w_down.at[:, unit_lanes(q)], wd.at[pl.ds(0, HALF), pl.ds(q * WIDTH, WIDTH)],
                              d_local.at[q]).start()

    squares = jnp.zeros((ROWS, WIDTH), F32)
    for q in range(NU):
        part = hidden[:, unit_lanes(q)].astype(F32)
        squares += part * part
    factor = lax.rsqrt(jnp.sum(squares, axis=1, keepdims=True) * (1.0 / D) + EPS)
    for q, (r, _) in enumerate(UNITS):
        lanes = unit_lanes(q)
        part = hidden[:, lanes].astype(F32) * factor * gain[:, lanes].astype(F32)
        g1[aligned(at[ORDERS[r][0]], 32), lanes] = part.astype(BF16)
    gate_v = gates[...]
    weight = gate_v / jnp.sum(gate_v, axis=1, keepdims=True)
    w_hi = weight.astype(BF16).astype(F32)
    w_lo = (weight - w_hi).astype(BF16).astype(F32)
    ids_f = ids[...].astype(F32)
    lane = lax.broadcasted_iota(jnp.int32, (ROWS, 128), 1)
    meta = jnp.zeros((ROWS, 128), F32)
    for i, part in enumerate((ids_f, w_hi, w_lo)):
        for k in range(TOP):
            meta = jnp.where(lane == i * TOP + k, part[:, k:k + 1], meta)
    meta = meta.astype(BF16)
    for r in range(3):
        a = at[ORDERS[r][0]]
        m1[r, aligned(a, 32), :] = meta

    pl.semaphore_wait(barrier, 10)

    for r in range(3):
        a = at[ORDERS[r][0]]
        for shift in (1, 2, 3):
            _, target = peer(ORDERS[r][0], shift)
            view = m1.at[r, aligned(a, 32), :]
            send(view, view, send_m, recv_m1.at[r], target)
    for q, (r, _) in enumerate(UNITS):
        a = at[ORDERS[r][0]]
        for shift in (1, 2, 3):
            _, target = peer(ORDERS[r][0], shift)
            view = g1.at[aligned(a, 32), unit_lanes(q)]
            send(view, view, send1, recv1.at[q], target)

    def send_other(src, dst, rsem):
        pltpu.make_async_remote_copy(
            src_ref=src, dst_ref=dst, send_sem=w_send, recv_sem=rsem,
            device_id=(1 - grp, dev), device_id_type=MESH,
        ).start()

    for i, (r, k0, kw, _) in enumerate(GROUPS):
        rows = pl.ds(k0, kw)
        send_other(w_gate.at[rows], w1.at[rows, pl.ds(HALF, HALF)], w_recv.at[i])
        send_other(w_up.at[rows], w1.at[rows, pl.ds(3 * HALF, HALF)], w_recv.at[i])
    send_other(w_down, down_other, d_recv)

    for r in range(3):
        b = at[ORDERS[r][1]]
        wait_bytes(m1.at[r, pl.ds(0, 96), :], recv_m1.at[r])
        for shift in (1, 2, 3):
            _, target = peer(ORDERS[r][1], shift)
            send(m1.at[r], m2.at[r, aligned(b, 128), :], send_m, recv_m2.at[r], target)
        m2[r, aligned(b, 128), :] = m1[r]
    for q, (r, _) in enumerate(UNITS):
        b = at[ORDERS[r][1]]
        lanes = unit_lanes(q)
        wait_bytes(g1.at[pl.ds(0, 96), lanes], recv1.at[q])
        for shift in (1, 2, 3):
            _, target = peer(ORDERS[r][1], shift)
            send(g1.at[:, lanes], g2.at[aligned(b, 128), lanes], send2, recv2.at[q], target)
        g2[aligned(b, 128), lanes] = g1[:, lanes]

    row_s = lax.broadcasted_iota(jnp.int32, (256, 256), 0)
    col_s = lax.broadcasted_iota(jnp.int32, (256, 256), 1)
    same = row_s // 32 == col_s // 32
    upper = jnp.where(same & (row_s < col_s), 1.0, 0.0).astype(BF16)
    lower = jnp.where(lax.broadcasted_iota(jnp.int32, (ROWS, ROWS), 0) > lax.broadcasted_iota(jnp.int32, (ROWS, ROWS), 1),
                      1.0, 0.0).astype(BF16)

    def experts_of(r):
        c_axis = ORDERS[r][2]
        return [(dev + (c - at[c_axis]) * STRIDE[c_axis]).astype(F32) for c in range(4)]

    def build_pick(r):
        for half in range(2):
            meta_t = jnp.transpose(m2[r, pl.ds(half * 256, 256), :].astype(F32))
            ids_t = meta_t[0:TOP]
            sub = lax.broadcasted_iota(jnp.int32, (8, 256), 0)
            block = lax.broadcasted_iota(jnp.int32, (8, 256), 1) // 32
            present = jnp.zeros((8, 256), F32)
            for c, e in enumerate(experts_of(r)):
                one = jnp.sum(jnp.where(ids_t == e, 1.0, 0.0), axis=0, keepdims=True)
                present = jnp.where(sub == c, one, present)
            slot = jnp.dot(present.astype(BF16), upper, preferred_element_type=F32)
            spot = jnp.where(present > 0.5, block.astype(F32) * 8.0 + slot, -1.0)
            index = lax.broadcasted_iota(jnp.int32, (64, 256), 0).astype(F32)
            for c in range(4):
                pick[r, half, pl.ds(c * 64, 64), :] = jnp.where(index == spot[c:c + 1], 1.0, 0.0).astype(BF16)

    def build_mix(r):
        lanes = lax.broadcasted_iota(jnp.int32, (ROWS, 128), 1)
        spots = lax.broadcasted_iota(jnp.int32, (ROWS, 256), 1)

        def one_block(n, carry):
            half, block = n // 8, n % 8
            table = m2[r, aligned(n, ROWS), :].astype(F32)
            shifted = jnp.where(lanes < TOP, table, -1.0)
            present = jnp.zeros((ROWS, 128), F32)
            his, los = [], []
            for c, e in enumerate(experts_of(r)):
                hit = jnp.where(shifted == e, 1.0, 0.0)
                present = jnp.where(lanes == c, jnp.sum(hit, axis=1, keepdims=True), present)
                his.append(jnp.sum(pltpu.roll(hit, TOP, 1) * table, axis=1, keepdims=True))
                los.append(jnp.sum(pltpu.roll(hit, 2 * TOP, 1) * table, axis=1, keepdims=True))
            slot = jnp.dot(lower, present.astype(BF16), preferred_element_type=F32)
            spot = jnp.full((ROWS, 256), -1.0, F32)
            hi = jnp.zeros((ROWS, 256), F32)
            lo = jnp.zeros((ROWS, 256), F32)
            base = (block * 8).astype(F32)
            for c in range(4):
                mine = spots // 64 == c
                where = jnp.where(present[:, c:c + 1] > 0.5, base + slot[:, c:c + 1], -1.0)
                spot = jnp.where(mine, where, spot)
                hi = jnp.where(mine, his[c], hi)
                lo = jnp.where(mine, los[c], lo)
            fits = (spots % 64).astype(F32) == spot
            mix[r, half, 0, aligned(block, ROWS), :] = jnp.where(fits, hi, 0.0).astype(BF16)
            mix[r, half, 1, aligned(block, ROWS), :] = jnp.where(fits, lo, 0.0).astype(BF16)
            return carry

        lax.fori_loop(0, 16, one_block, 0)

    for q, (r, j) in enumerate(UNITS):
        c_at = at[ORDERS[r][2]]
        lanes = unit_lanes(q)
        if j == 0:
            wait_bytes(m2.at[r, pl.ds(0, 384), :], recv_m2.at[r])
            build_pick(r)
        wait_bytes(g2.at[pl.ds(0, 384), lanes], recv2.at[q])
        for half in range(2):
            v = jnp.dot(pick[r, half], g2[pl.ds(half * 256, 256), lanes], preferred_element_type=F32).astype(BF16)
            for c in range(4):
                sel[pl.ds(c * 128 + half * 64, 64), lanes] = v[c * 64:c * 64 + 64]
        for shift in (1, 2, 3):
            other, target = peer(ORDERS[r][2], shift)
            send(sel.at[aligned(other, 128), lanes], xs.at[aligned(c_at, 128), lanes], send3, recv3.at[q], target)
        xs[aligned(c_at, 128), lanes] = sel[aligned(c_at, 128), lanes]
    for r in range(3):
        build_mix(r)

    for i, (r, k0, kw, units) in enumerate(GROUPS):
        rows = pl.ds(k0, kw)
        for q in units:
            wait_bytes(xs.at[pl.ds(0, 384), unit_lanes(q)], recv3.at[q])
        wait_bytes(w1.at[rows, pl.ds(0, 2 * HALF)], w_local.at[i])
        wait_bytes(w1.at[rows, pl.ds(0, 2 * HALF)], w_recv.at[i])
        where = tile_map(r)

        def step(n, carry, r=r, rows=rows, first=(i == 0), where=where):
            cols = pl.ds(pl.multiple_of(n * 256, 256), 256)
            res = jnp.dot(xs[:, rows], w1[rows, cols], preferred_element_type=F32)
            if first:
                acc[:, cols] = res
            elif r == 0:
                acc[:, cols] += res
            else:
                for p in range(64):
                    acc[pl.ds(where[p] * 8, 8), cols] += res[p * 8:p * 8 + 8]
            return carry

        lax.fori_loop(0, 4 * HALF // 256, step, 0)
        if i == FREED:
            wait_bytes(down_other, d_recv)
            for q in range(EARLY):
                pltpu.make_async_copy(down_other.at[:, unit_lanes(q)],
                                      wd.at[pl.ds(HALF, HALF), pl.ds(q * WIDTH, WIDTH)], d_local.at[q]).start()
            for q in range(EARLY, NU):
                cols = pl.ds((q - EARLY) * WIDTH, WIDTH)
                pltpu.make_async_copy(w_down.at[:, unit_lanes(q)], w1.at[pl.ds(0, HALF), cols], d_local.at[q]).start()
                pltpu.make_async_copy(down_other.at[:, unit_lanes(q)], w1.at[pl.ds(HALF, HALF), cols],
                                      d_local.at[q]).start()

    def activate(n, carry):
        rows = aligned(n, 32)
        v = acc[rows, 0:2 * HALF]
        act[rows, :] = (v / (1.0 + jnp.exp(-v)) * acc[rows, 2 * HALF:4 * HALF]).astype(BF16)
        return carry

    lax.fori_loop(0, 16, activate, 0)

    wait_bytes(sel.at[pl.ds(0, 384), :], send3)
    wait_bytes(g1.at[pl.ds(0, 96), :], send1)
    wait_bytes(g2.at[pl.ds(0, 384), :], send2)

    for q, (r, j) in enumerate(UNITS):
        c_at = at[ORDERS[r][2]]
        lanes = unit_lanes(q)
        if q < EARLY:
            down = wd.at[:, pl.ds(q * WIDTH, WIDTH)]
        else:
            down = w1.at[pl.ds(0, 2 * HALF), pl.ds((q - EARLY) * WIDTH, WIDTH)]
        wait_bytes(down, d_local.at[q])
        res = jnp.dot(act[...], down[...], preferred_element_type=F32)
        where = tile_map(r)
        for p in range(0, 64, 2):
            pair = jnp.concatenate([res[where[p + i] * 8:where[p + i] * 8 + 8] for i in range(2)], axis=0)
            sel[pl.ds(p * 8, 16), lanes] = pair.astype(BF16)
        for shift in (1, 2, 3):
            other, target = peer(ORDERS[r][2], shift)
            send(sel.at[aligned(other, 128), lanes], g2.at[aligned(c_at, 128), lanes], send_c, recv_c.at[q], target)
        g2[aligned(c_at, 128), lanes] = sel[aligned(c_at, 128), lanes]

    for q, (r, j) in enumerate(UNITS):
        b = at[ORDERS[r][1]]
        lanes = unit_lanes(q)
        wait_bytes(g2.at[pl.ds(0, 384), lanes], recv_c.at[q])
        for half in range(2):
            v = jnp.concatenate([g2[pl.ds(m * 128 + half * 64, 64), lanes] for m in range(4)], axis=0)
            total = jnp.dot(mix[r, half, 0], v, preferred_element_type=F32)
            total += jnp.dot(mix[r, half, 1], v, preferred_element_type=F32)
            xs[pl.ds(half * 256, 256), lanes] = total.astype(BF16)
        for shift in (1, 2, 3):
            other, target = peer(ORDERS[r][1], shift)
            send(xs.at[aligned(other, 128), lanes], rb.at[aligned(b, 128), lanes], send_b, recv_b.at[q], target)
        rb[aligned(b, 128), lanes] = xs[aligned(b, 128), lanes]

    for q, (r, j) in enumerate(UNITS):
        a = at[ORDERS[r][0]]
        lanes = unit_lanes(q)
        wait_bytes(rb.at[pl.ds(0, 384), lanes], recv_b.at[q])
        total = rb[pl.ds(0, 128), lanes].astype(F32)
        for m in range(1, 4):
            total += rb[pl.ds(m * 128, 128), lanes].astype(F32)
        g1[:, lanes] = total.astype(BF16)
        for shift in (1, 2, 3):
            other, target = peer(ORDERS[r][0], shift)
            send(g1.at[aligned(other, 32), lanes], ra.at[aligned(a, 32), lanes], send_a, recv_a.at[q], target)
        ra[aligned(a, 32), lanes] = g1[aligned(a, 32), lanes]

    for q in range(NU):
        lanes = unit_lanes(q)
        wait_bytes(ra.at[pl.ds(0, 96), lanes], recv_a.at[q])
        total = ra[pl.ds(0, 32), lanes].astype(F32)
        for m in range(1, 4):
            total += ra[pl.ds(m * 32, 32), lanes].astype(F32)
        out[:, lanes] = (hidden[:, lanes].astype(F32) + total).astype(BF16)

    wait_bytes(m1.at[:, pl.ds(0, 96), :], send_m)
    wait_bytes(m2.at[:, pl.ds(0, 384), :], send_m)
    wait_bytes(w1.at[:, pl.ds(0, 2 * HALF)], w_send)
    wait_bytes(down_other, w_send)
    wait_bytes(sel.at[pl.ds(0, 384), :], send_c)
    wait_bytes(xs.at[pl.ds(0, 384), :], send_b)
    wait_bytes(g1.at[pl.ds(0, 96), :], send_a)


def local(hidden, norm_gain, expert_ids, gate_values, w_gate, w_up, w_down):
    vmem = pl.BlockSpec(memory_space=pltpu.VMEM)
    anywhere = pl.BlockSpec(memory_space=pl.ANY)
    dma = pltpu.SemaphoreType.DMA
    buf = pltpu.VMEM
    out, _ = pl.pallas_call(
        body,
        out_shape=(
            jax.ShapeDtypeStruct((ROWS, D), BF16),
            jax.ShapeDtypeStruct((HALF, D), BF16),
        ),
        in_specs=[vmem] * 4 + [anywhere] * 3,
        out_specs=(vmem, anywhere),
        scratch_shapes=[
            buf((128, D), BF16), buf((512, D), BF16), buf((512, D), BF16), buf((512, D), BF16),
            buf((512, D), BF16), buf((128, D), BF16),
            buf((512, 4 * HALF), F32), buf((512, 2 * HALF), BF16),
            buf((D, 4 * HALF), BF16), buf((2 * HALF, EARLY * WIDTH), BF16),
            buf((3, 128, 128), BF16), buf((3, 512, 128), BF16),
            buf((3, 2, 256, 256), BF16), buf((3, 2, 2, 256, 256), BF16),
        ] + [dma((NU,))] * 6 + [dma((3,))] * 2 + [dma] * 7 + [
            dma((len(GROUPS),)), dma((len(GROUPS),)), dma, dma, dma((NU,)),
        ],
        compiler_params=pltpu.CompilerParams(
            collective_id=0, has_side_effects=True, vmem_limit_bytes=60 * 2**20
        ),
        name="expert_layer",
    )(hidden, norm_gain.reshape(1, D), expert_ids, gate_values, w_gate[0], w_up[0], w_down[0])
    return out


def solution(mesh):
    return jax.shard_map(
        local,
        mesh=mesh,
        in_specs=(
            P(("grp", "dev"), None),
            P(),
            P(("grp", "dev"), None),
            P(("grp", "dev"), None),
            P("dev", None, "grp"),
            P("dev", None, "grp"),
            P("dev", "grp", None),
        ),
        out_specs=P(("grp", "dev"), None),
        check_vma=False,
    )
```

```python
import functools

import jax
import jax.numpy as jnp
from jax import lax
from jax.experimental import pallas as pl
from jax.experimental.pallas import tpu as pltpu
from jax.sharding import PartitionSpec as P

D = 4096
HALF = 768
TOP = 8
ROWS = 32
EPS = 1e-06
MESH = pl.DeviceIdType.MESH
F32, BF16 = jnp.float32, jnp.bfloat16

ORDERS = (("y", "z", "x"), ("z", "x", "y"), ("x", "y", "z"))
STRIDE = {"y": 16, "z": 4, "x": 1}
COUNT = (6, 5, 5)
BASE = (0, 1536, 2816)
WIDTH = 256
UNITS = [(r, j) for j in range(6) for r in range(3) if j < COUNT[r]]
NU = len(UNITS)
GROUPS = []
for _i, _order in enumerate(((0, 1, 2), (0, 1, 2), (1, 2, 0))):
    for _r in _order:
        _js = [j for j in (2 * _i, 2 * _i + 1) if j < COUNT[_r]]
        GROUPS.append((_r, BASE[_r] + _js[0] * WIDTH, len(_js) * WIDTH, [UNITS.index((_r, j)) for j in _js]))
FREED = max(i for i, grp in enumerate(GROUPS) if grp[0] == 1)
LATER = BASE[1]
EARLY = 4
CHUNK = 1536
LAST = 512


def tile_map(r):
    out = []
    for p in range(64):
        at = dict(zip(ORDERS[r], (p % 4, p // 4 % 4, p // 16)))
        out.append(at[ORDERS[0][2]] * 16 + at[ORDERS[0][1]] * 4 + at[ORDERS[0][0]])
    return out


def unit_lanes(q):
    r, j = UNITS[q]
    return pl.ds(BASE[r] + j * WIDTH, WIDTH)


def aligned(index, rows):
    return pl.ds(pl.multiple_of(index * rows, rows), rows)


def wait_bytes(view, sem):
    pltpu.make_async_copy(view, view, sem).wait()


def body(hidden, gain, ids, gates, w_gate, w_up, w_down, out, down_other,
         g1, g2, sel, xs, rb, ra, acc, act, w1, wd, m1, m2, pick, mix,
         recv1, recv2, recv3, recv_c, recv_b, recv_a, recv_m1, recv_m2,
         send1, send2, send3, send_c, send_b, send_a, send_m,
         w_local, w_recv, w_send, d_recv, d_local):
    grp = lax.axis_index("grp")
    dev = lax.axis_index("dev")
    at = {"y": dev // 16, "z": (dev // 4) % 4, "x": dev % 4}

    def peer(axis, shift):
        other = (at[axis] + shift) % 4
        return other, dev + (other - at[axis]) * STRIDE[axis]

    def send(src, dst, ssem, rsem, target):
        pltpu.make_async_remote_copy(
            src_ref=src, dst_ref=dst, send_sem=ssem, recv_sem=rsem,
            device_id=(grp, target), device_id_type=MESH,
        ).start()

    barrier = pltpu.get_barrier_semaphore()
    for axis in ("y", "z", "x"):
        for shift in (1, 2, 3):
            _, target = peer(axis, shift)
            pl.semaphore_signal(barrier, inc=1, device_id=(grp, target), device_id_type=MESH)
    pl.semaphore_signal(barrier, inc=1, device_id=(1 - grp, dev), device_id_type=MESH)

    for i, (r, k0, kw, _) in enumerate(GROUPS):
        rows = pl.ds(k0, kw)
        pltpu.make_async_copy(w_gate.at[rows], w1.at[rows, pl.ds(0, HALF)], w_local.at[i]).start()
        pltpu.make_async_copy(w_up.at[rows], w1.at[rows, pl.ds(2 * HALF, HALF)], w_local.at[i]).start()
    for q in range(EARLY):
        pltpu.make_async_copy(w_down.at[:, unit_lanes(q)], wd.at[pl.ds(0, HALF), pl.ds(q * WIDTH, WIDTH)],
                              d_local.at[q]).start()

    squares = jnp.zeros((ROWS, WIDTH), F32)
    for q in range(NU):
        part = hidden[:, unit_lanes(q)].astype(F32)
        squares += part * part
    factor = lax.rsqrt(jnp.sum(squares, axis=1, keepdims=True) * (1.0 / D) + EPS)
    for q, (r, _) in enumerate(UNITS):
        lanes = unit_lanes(q)
        row = (BASE[r] + UNITS[q][1] * WIDTH) // 128
        scale = jnp.concatenate([gain[row + i:row + i + 1, :] for i in range(WIDTH // 128)], axis=1).astype(F32)
        part = hidden[:, lanes].astype(F32) * factor * scale
        g1[aligned(at[ORDERS[r][0]], 32), lanes] = part.astype(BF16)
    gate_v = gates[...]
    weight = gate_v / jnp.sum(gate_v, axis=0, keepdims=True)
    w_hi = weight.astype(BF16).astype(F32)
    routing = jnp.concatenate([ids[...].astype(F32), w_hi, weight - w_hi, jnp.zeros((TOP, ROWS), F32)], axis=0)
    eye = jnp.where(lax.broadcasted_iota(jnp.int32, (4 * TOP, 128), 0) == lax.broadcasted_iota(jnp.int32, (4 * TOP, 128), 1),
                    1.0, 0.0).astype(BF16)
    meta = lax.dot_general(routing.astype(BF16), eye, (((0,), (0,)), ((), ())), preferred_element_type=F32).astype(BF16)
    for r in range(3):
        a = at[ORDERS[r][0]]
        m1[r, aligned(a, 32), :] = meta

    pl.semaphore_wait(barrier, 10)

    for r in range(3):
        a = at[ORDERS[r][0]]
        for shift in (1, 2, 3):
            _, target = peer(ORDERS[r][0], shift)
            view = m1.at[r, aligned(a, 32), :]
            send(view, view, send_m, recv_m1.at[r], target)
    for q, (r, _) in enumerate(UNITS):
        a = at[ORDERS[r][0]]
        for shift in (1, 2, 3):
            _, target = peer(ORDERS[r][0], shift)
            view = g1.at[aligned(a, 32), unit_lanes(q)]
            send(view, view, send1, recv1.at[q], target)

    def send_other(src, dst, rsem):
        pltpu.make_async_remote_copy(
            src_ref=src, dst_ref=dst, send_sem=w_send, recv_sem=rsem,
            device_id=(1 - grp, dev), device_id_type=MESH,
        ).start()

    def send_weights(i):
        if i < len(GROUPS):
            rows = pl.ds(GROUPS[i][1], GROUPS[i][2])
            send_other(w_gate.at[rows], w1.at[rows, pl.ds(HALF, HALF)], w_recv.at[i])
            send_other(w_up.at[rows], w1.at[rows, pl.ds(3 * HALF, HALF)], w_recv.at[i])
        elif i == len(GROUPS):
            send_other(w_down, down_other, d_recv)

    for q, (r, j) in enumerate(UNITS):
        b = at[ORDERS[r][1]]
        lanes = unit_lanes(q)
        wait_bytes(g1.at[pl.ds(0, 96), lanes], recv1.at[q])
        for shift in (1, 2, 3):
            _, target = peer(ORDERS[r][1], shift)
            send(g1.at[:, lanes], g2.at[aligned(b, 128), lanes], send2, recv2.at[q], target)
        g2[aligned(b, 128), lanes] = g1[:, lanes]
        if j == 0:
            wait_bytes(m1.at[r, pl.ds(0, 96), :], recv_m1.at[r])
            for shift in (1, 2, 3):
                _, target = peer(ORDERS[r][1], shift)
                send(m1.at[r], m2.at[r, aligned(b, 128), :], send_m, recv_m2.at[r], target)
            m2[r, aligned(b, 128), :] = m1[r]
        send_weights(q)

    row_s = lax.broadcasted_iota(jnp.int32, (256, 256), 0)
    col_s = lax.broadcasted_iota(jnp.int32, (256, 256), 1)
    upper = jnp.where((row_s // 32 == col_s // 32) & (row_s < col_s), 1.0, 0.0).astype(BF16)
    index = lax.broadcasted_iota(jnp.int32, (64, 256), 0).astype(F32)

    def routes(r, half):
        meta_t = jnp.transpose(m2[r, pl.ds(half * 256, 256), :].astype(F32))
        ids_t, hi_t, lo_t = (meta_t[i * TOP:i * TOP + TOP] for i in range(3))
        sub = lax.broadcasted_iota(jnp.int32, (8, 256), 0)
        block = (lax.broadcasted_iota(jnp.int32, (8, 256), 1) // 32).astype(F32)
        present = jnp.zeros((8, 256), F32)
        terms = []
        c_axis = ORDERS[r][2]
        for c in range(4):
            expert = (dev + (c - at[c_axis]) * STRIDE[c_axis]).astype(F32)
            hit = ids_t == expert
            present = jnp.where(sub == c, jnp.sum(jnp.where(hit, 1.0, 0.0), axis=0, keepdims=True), present)
            terms.append([jnp.sum(jnp.where(hit, t, 0.0), axis=0, keepdims=True) for t in (hi_t, lo_t)])
        slot = jnp.dot(present.astype(BF16), upper, preferred_element_type=F32)
        return jnp.where(present > 0.5, block * 8.0 + slot, -1.0), terms

    def build_pick(r):
        for half in range(2):
            spot, _ = routes(r, half)
            for c in range(4):
                pick[r, half, pl.ds(c * 64, 64), :] = jnp.where(index == spot[c:c + 1], 1.0, 0.0).astype(BF16)

    def build_mix(r):
        for half in range(2):
            spot, terms = routes(r, half)
            for i in range(2):
                table = jnp.concatenate([jnp.where(index == spot[c:c + 1], terms[c][i], 0.0) for c in range(4)], axis=0)
                mix[r, half, i] = jnp.transpose(table).astype(BF16)

    for q, (r, j) in enumerate(UNITS):
        c_at = at[ORDERS[r][2]]
        lanes = unit_lanes(q)
        if j == 0:
            wait_bytes(m2.at[r, pl.ds(0, 384), :], recv_m2.at[r])
            build_pick(r)
        wait_bytes(g2.at[pl.ds(0, 384), lanes], recv2.at[q])
        for half in range(2):
            v = jnp.dot(pick[r, half], g2[pl.ds(half * 256, 256), lanes], preferred_element_type=F32).astype(BF16)
            for c in range(4):
                sel[pl.ds(c * 128 + half * 64, 64), lanes] = v[c * 64:c * 64 + 64]
        for shift in (1, 2, 3):
            other, target = peer(ORDERS[r][2], shift)
            send(sel.at[aligned(other, 128), lanes], xs.at[aligned(c_at, 128), lanes], send3, recv3.at[q], target)
        xs[aligned(c_at, 128), lanes] = sel[aligned(c_at, 128), lanes]
    for r in range(3):
        build_mix(r)

    for i, (r, k0, kw, units) in enumerate(GROUPS):
        rows = pl.ds(k0, kw)
        for q in units:
            wait_bytes(xs.at[pl.ds(0, 384), unit_lanes(q)], recv3.at[q])
        wait_bytes(w1.at[rows, pl.ds(0, 2 * HALF)], w_local.at[i])
        wait_bytes(w1.at[rows, pl.ds(0, 2 * HALF)], w_recv.at[i])
        where = tile_map(r)

        if i < len(GROUPS) - 1:
            def step(n, carry, r=r, rows=rows, first=(i == 0), where=where):
                cols = pl.ds(pl.multiple_of(n * CHUNK, CHUNK), CHUNK)
                res = jnp.dot(xs[:, rows], w1[rows, cols], preferred_element_type=F32)
                if first:
                    acc[:, cols] = res
                elif r == 0:
                    acc[:, cols] += res
                else:
                    for p in range(64):
                        acc[pl.ds(where[p] * 8, 8), cols] += res[p * 8:p * 8 + 8]
                return carry

            lax.fori_loop(0, 4 * HALF // CHUNK, step, 0)
        else:
            def last(n, carry, rows=rows):
                at_gate = pl.ds(pl.multiple_of(n * LAST, LAST), LAST)
                at_up = pl.ds(pl.multiple_of(2 * HALF + n * LAST, LAST), LAST)
                v = acc[:, at_gate] + jnp.dot(xs[:, rows], w1[rows, at_gate], preferred_element_type=F32)
                u = acc[:, at_up] + jnp.dot(xs[:, rows], w1[rows, at_up], preferred_element_type=F32)
                act[:, at_gate] = (v / (1.0 + jnp.exp(-v)) * u).astype(BF16)
                return carry

            lax.fori_loop(0, 2 * HALF // LAST, last, 0)
        if i == FREED:
            wait_bytes(down_other, d_recv)
            for q in range(EARLY):
                pltpu.make_async_copy(down_other.at[:, unit_lanes(q)],
                                      wd.at[pl.ds(HALF, HALF), pl.ds(q * WIDTH, WIDTH)], d_local.at[q]).start()
            for q in range(EARLY, NU):
                cols = pl.ds((q - EARLY) * WIDTH, WIDTH)
                pltpu.make_async_copy(w_down.at[:, unit_lanes(q)], w1.at[pl.ds(LATER, HALF), cols], d_local.at[q]).start()
                pltpu.make_async_copy(down_other.at[:, unit_lanes(q)], w1.at[pl.ds(LATER + HALF, HALF), cols],
                                      d_local.at[q]).start()

    wait_bytes(sel.at[pl.ds(0, 384), :], send3)
    wait_bytes(g1.at[pl.ds(0, 96), :], send1)
    wait_bytes(g2.at[pl.ds(0, 384), :], send2)

    for q, (r, j) in enumerate(UNITS):
        c_at = at[ORDERS[r][2]]
        lanes = unit_lanes(q)
        if q < EARLY:
            down = wd.at[:, pl.ds(q * WIDTH, WIDTH)]
        else:
            down = w1.at[pl.ds(LATER, 2 * HALF), pl.ds((q - EARLY) * WIDTH, WIDTH)]
        wait_bytes(down, d_local.at[q])
        res = jnp.dot(act[...], down[...], preferred_element_type=F32)
        where = tile_map(r)
        for p in range(0, 64, 2):
            pair = jnp.concatenate([res[where[p + i] * 8:where[p + i] * 8 + 8] for i in range(2)], axis=0)
            sel[pl.ds(p * 8, 16), lanes] = pair.astype(BF16)
        for shift in (1, 2, 3):
            other, target = peer(ORDERS[r][2], shift)
            send(sel.at[aligned(other, 128), lanes], g2.at[aligned(c_at, 128), lanes], send_c, recv_c.at[q], target)
        g2[aligned(c_at, 128), lanes] = sel[aligned(c_at, 128), lanes]

    for q, (r, j) in enumerate(UNITS):
        b = at[ORDERS[r][1]]
        lanes = unit_lanes(q)
        wait_bytes(g2.at[pl.ds(0, 384), lanes], recv_c.at[q])
        for half in range(2):
            v = jnp.concatenate([g2[pl.ds(m * 128 + half * 64, 64), lanes] for m in range(4)], axis=0)
            total = jnp.dot(mix[r, half, 0], v, preferred_element_type=F32)
            total += jnp.dot(mix[r, half, 1], v, preferred_element_type=F32)
            xs[pl.ds(half * 256, 256), lanes] = total.astype(BF16)
        for shift in (1, 2, 3):
            other, target = peer(ORDERS[r][1], shift)
            send(xs.at[aligned(other, 128), lanes], rb.at[aligned(b, 128), lanes], send_b, recv_b.at[q], target)
        rb[aligned(b, 128), lanes] = xs[aligned(b, 128), lanes]

    for q, (r, j) in enumerate(UNITS):
        a = at[ORDERS[r][0]]
        lanes = unit_lanes(q)
        wait_bytes(rb.at[pl.ds(0, 384), lanes], recv_b.at[q])
        total = rb[pl.ds(0, 128), lanes].astype(F32)
        for m in range(1, 4):
            total += rb[pl.ds(m * 128, 128), lanes].astype(F32)
        g1[:, lanes] = total.astype(BF16)
        for shift in (1, 2, 3):
            other, target = peer(ORDERS[r][0], shift)
            send(g1.at[aligned(other, 32), lanes], ra.at[aligned(a, 32), lanes], send_a, recv_a.at[q], target)
        ra[aligned(a, 32), lanes] = g1[aligned(a, 32), lanes]

    for q in range(NU):
        lanes = unit_lanes(q)
        wait_bytes(ra.at[pl.ds(0, 96), lanes], recv_a.at[q])
        total = ra[pl.ds(0, 32), lanes].astype(F32)
        for m in range(1, 4):
            total += ra[pl.ds(m * 32, 32), lanes].astype(F32)
        out[:, lanes] = (hidden[:, lanes].astype(F32) + total).astype(BF16)

    wait_bytes(m1.at[:, pl.ds(0, 96), :], send_m)
    wait_bytes(m2.at[:, pl.ds(0, 384), :], send_m)
    wait_bytes(w1.at[:, pl.ds(0, 2 * HALF)], w_send)
    wait_bytes(down_other, w_send)
    wait_bytes(sel.at[pl.ds(0, 384), :], send_c)
    wait_bytes(xs.at[pl.ds(0, 384), :], send_b)
    wait_bytes(g1.at[pl.ds(0, 96), :], send_a)


def local(hidden, norm_gain, expert_ids, gate_values, w_gate, w_up, w_down):
    vmem = pl.BlockSpec(memory_space=pltpu.VMEM)
    anywhere = pl.BlockSpec(memory_space=pl.ANY)
    dma = pltpu.SemaphoreType.DMA
    buf = pltpu.VMEM
    out, _ = pl.pallas_call(
        body,
        out_shape=(
            jax.ShapeDtypeStruct((ROWS, D), BF16),
            jax.ShapeDtypeStruct((HALF, D), BF16),
        ),
        in_specs=[vmem] * 4 + [anywhere] * 3,
        out_specs=(vmem, anywhere),
        scratch_shapes=[
            buf((128, D), BF16), buf((512, D), BF16), buf((512, D), BF16), buf((512, D), BF16),
            buf((512, D), BF16), buf((128, D), BF16),
            buf((512, 4 * HALF), F32), buf((512, 2 * HALF), BF16),
            buf((D, 4 * HALF), BF16), buf((2 * HALF, EARLY * WIDTH), BF16),
            buf((3, 128, 128), BF16), buf((3, 512, 128), BF16),
            buf((3, 2, 256, 256), BF16), buf((3, 2, 2, 256, 256), BF16),
        ] + [dma((NU,))] * 6 + [dma((3,))] * 2 + [dma] * 7 + [
            dma((len(GROUPS),)), dma((len(GROUPS),)), dma, dma, dma((NU,)),
        ],
        compiler_params=pltpu.CompilerParams(
            collective_id=0, has_side_effects=True, vmem_limit_bytes=60 * 2**20
        ),
        name="expert_layer",
    )(hidden, norm_gain.reshape(D // 128, 128), expert_ids.T, gate_values.T, w_gate[0], w_up[0], w_down[0])
    return out


def solution(mesh):
    return jax.shard_map(
        local,
        mesh=mesh,
        in_specs=(
            P(("grp", "dev"), None),
            P(),
            P(("grp", "dev"), None),
            P(("grp", "dev"), None),
            P("dev", None, "grp"),
            P("dev", None, "grp"),
            P("dev", "grp", None),
        ),
        out_specs=P(("grp", "dev"), None),
        check_vma=False,
    )
```

```python
import functools

import jax
import jax.numpy as jnp
from jax import lax
from jax.experimental import pallas as pl
from jax.experimental.pallas import tpu as pltpu
from jax.sharding import PartitionSpec as P

D = 4096
HALF = 768
TOP = 8
ROWS = 32
EPS = 1e-06
MESH = pl.DeviceIdType.MESH
F32, BF16 = jnp.float32, jnp.bfloat16

ORDERS = (("y", "z", "x"), ("z", "x", "y"), ("x", "y", "z"))
STRIDE = {"y": 16, "z": 4, "x": 1}
COUNT = (6, 5, 5)
BASE = (0, 1536, 2816)
WIDTH = 256
UNITS = [(r, j) for j in range(6) for r in range(3) if j < COUNT[r]]
NU = len(UNITS)
GROUPS = []
for _i, _order in enumerate(((0, 1, 2), (0, 1, 2), (1, 2, 0))):
    for _r in _order:
        _js = [j for j in (2 * _i, 2 * _i + 1) if j < COUNT[_r]]
        GROUPS.append((_r, BASE[_r] + _js[0] * WIDTH, len(_js) * WIDTH, [UNITS.index((_r, j)) for j in _js]))
FREED = max(i for i, grp in enumerate(GROUPS) if grp[0] == 1)
LATER = BASE[1]
EARLY = 4
BLOCK = 1024
BLOCK_AT = [BASE[r] + UNITS[:EARLY].count((r, 0)) * WIDTH + UNITS[:EARLY].count((r, 1)) * WIDTH for r in range(3)]
LAG = 6
BETWEEN = ()
BACK = (0, 16, 32, 48, 64)
CHUNK = 1536
LAST = 512


def tile_map(r):
    out = []
    for p in range(64):
        at = dict(zip(ORDERS[r], (p % 4, p // 4 % 4, p // 16)))
        out.append(at[ORDERS[0][2]] * 16 + at[ORDERS[0][1]] * 4 + at[ORDERS[0][0]])
    return out


def unit_lanes(q):
    r, j = UNITS[q]
    return pl.ds(BASE[r] + j * WIDTH, WIDTH)


def half_lanes(q, i):
    r, j = UNITS[q]
    return pl.ds(BASE[r] + j * WIDTH + i * (WIDTH // 2), WIDTH // 2)


def aligned(index, rows):
    return pl.ds(pl.multiple_of(index * rows, rows), rows)


def wait_bytes(view, sem):
    pltpu.make_async_copy(view, view, sem).wait()


def body(hidden, gain, ids, gates, w_gate, w_up, w_down, out, down_other,
         g1, g2, sel, xs, rt, rb, ra, acc, act, w1, wd, m1, m2, pick, mix,
         recv1, recv_up, recv_dn, recv_far, recv3, recv_c, recv_t, recv_b, recv_a, send_far,
         recv_m1, recv_m2, send1, send2, send3, send_c, send_t, send_b, send_a, send_m,
         w_local, w_recv, w_send, d_recv, d_local):
    grp = lax.axis_index("grp")
    dev = lax.axis_index("dev")
    at = {"y": dev // 16, "z": (dev // 4) % 4, "x": dev % 4}

    def apart(step, q):
        def once(_, carry):
            step(q)
            return carry

        lax.fori_loop(0, 1 + dev // 64, once, 0)

    def peer(axis, shift):
        other = (at[axis] + shift) % 4
        return other, dev + (other - at[axis]) * STRIDE[axis]

    def send(src, dst, ssem, rsem, target):
        pltpu.make_async_remote_copy(
            src_ref=src, dst_ref=dst, send_sem=ssem, recv_sem=rsem,
            device_id=(grp, target), device_id_type=MESH,
        ).start()

    barrier = pltpu.get_barrier_semaphore()
    for axis in ("y", "z", "x"):
        for shift in (1, 2, 3):
            _, target = peer(axis, shift)
            pl.semaphore_signal(barrier, inc=1, device_id=(grp, target), device_id_type=MESH)
    pl.semaphore_signal(barrier, inc=1, device_id=(1 - grp, dev), device_id_type=MESH)

    for i, (r, k0, kw, _) in enumerate(GROUPS):
        rows = pl.ds(k0, kw)
        pltpu.make_async_copy(w_gate.at[rows], w1.at[rows, pl.ds(0, HALF)], w_local.at[i]).start()
        pltpu.make_async_copy(w_up.at[rows], w1.at[rows, pl.ds(2 * HALF, HALF)], w_local.at[i]).start()
    for q in range(EARLY):
        pltpu.make_async_copy(w_down.at[:, unit_lanes(q)], wd.at[pl.ds(0, HALF), pl.ds(q * WIDTH, WIDTH)],
                              d_local.at[q]).start()

    squares = jnp.zeros((ROWS, WIDTH), F32)
    for q in range(NU):
        part = hidden[:, unit_lanes(q)].astype(F32)
        squares += part * part
    factor = lax.rsqrt(jnp.sum(squares, axis=1, keepdims=True) * (1.0 / D) + EPS)
    for q, (r, _) in enumerate(UNITS):
        lanes = unit_lanes(q)
        row = (BASE[r] + UNITS[q][1] * WIDTH) // 128
        scale = jnp.concatenate([gain[row + i:row + i + 1, :] for i in range(WIDTH // 128)], axis=1).astype(F32)
        part = hidden[:, lanes].astype(F32) * factor * scale
        g1[aligned(at[ORDERS[r][0]], 32), lanes] = part.astype(BF16)
    gate_v = gates[...]
    weight = gate_v / jnp.sum(gate_v, axis=0, keepdims=True)
    w_hi = weight.astype(BF16).astype(F32)
    routing = jnp.concatenate([ids[...].astype(F32), w_hi, weight - w_hi, jnp.zeros((TOP, ROWS), F32)], axis=0)
    eye = jnp.where(lax.broadcasted_iota(jnp.int32, (4 * TOP, 128), 0) == lax.broadcasted_iota(jnp.int32, (4 * TOP, 128), 1),
                    1.0, 0.0).astype(BF16)
    meta = lax.dot_general(routing.astype(BF16), eye, (((0,), (0,)), ((), ())), preferred_element_type=F32).astype(BF16)
    for r in range(3):
        a = at[ORDERS[r][0]]
        m1[r, aligned(a, 32), :] = meta

    pl.semaphore_wait(barrier, 10)

    for r in range(3):
        a = at[ORDERS[r][0]]
        for shift in (1, 2, 3):
            _, target = peer(ORDERS[r][0], shift)
            view = m1.at[r, aligned(a, 32), :]
            send(view, view, send_m, recv_m1.at[r], target)
    for q, (r, _) in enumerate(UNITS):
        a = at[ORDERS[r][0]]
        for shift in (1, 2, 3):
            _, target = peer(ORDERS[r][0], shift)
            view = g1.at[aligned(a, 32), unit_lanes(q)]
            send(view, view, send1, recv1.at[q], target)

    def send_other(src, dst, rsem):
        pltpu.make_async_remote_copy(
            src_ref=src, dst_ref=dst, send_sem=w_send, recv_sem=rsem,
            device_id=(1 - grp, dev), device_id_type=MESH,
        ).start()

    def send_weights(i):
        if i < len(GROUPS):
            rows = pl.ds(GROUPS[i][1], GROUPS[i][2])
            send_other(w_gate.at[rows], w1.at[rows, pl.ds(HALF, HALF)], w_recv.at[i])
            send_other(w_up.at[rows], w1.at[rows, pl.ds(3 * HALF, HALF)], w_recv.at[i])
        elif i == len(GROUPS):
            send_other(w_down, down_other, d_recv)

    def stage_b(q):
        r, j = UNITS[q]
        axis = ORDERS[r][1]
        b = at[axis]
        lanes = unit_lanes(q)
        wait_bytes(g1.at[pl.ds(0, 96), lanes], recv1.at[q])
        for shift, sem in ((1, recv_up), (3, recv_dn)):
            _, target = peer(axis, shift)
            send(g1.at[:, lanes], g2.at[aligned(b, 128), lanes], send2, sem.at[q], target)
        g2[aligned(b, 128), lanes] = g1[:, lanes]
        if j == 0:
            wait_bytes(m1.at[r, pl.ds(0, 96), :], recv_m1.at[r])
            for shift in (1, 2, 3):
                _, target = peer(axis, shift)
                send(m1.at[r], m2.at[r, aligned(b, 128), :], send_m, recv_m2.at[r], target)
            m2[r, aligned(b, 128), :] = m1[r]
        send_weights(q)

    def pass_on(q):
        axis = ORDERS[UNITS[q][0]][1]
        for i, (shift, sem) in enumerate(((1, recv_up), (3, recv_dn))):
            came, _ = peer(axis, 4 - shift)
            _, target = peer(axis, shift)
            wait_bytes(g2.at[aligned(came, 128), unit_lanes(q)], sem.at[q])
            view = g2.at[aligned(came, 128), half_lanes(q, i)]
            send(view, view, send_far.at[q], recv_far.at[q], target)

    for t in range(NU + LAG):
        if t < NU:
            stage_b(t)
        if t >= LAG:
            pass_on(t - LAG)

    row_s = lax.broadcasted_iota(jnp.int32, (256, 256), 0)
    col_s = lax.broadcasted_iota(jnp.int32, (256, 256), 1)
    upper = jnp.where((row_s // 32 == col_s // 32) & (row_s < col_s), 1.0, 0.0).astype(BF16)
    index = lax.broadcasted_iota(jnp.int32, (64, 256), 0).astype(F32)

    def routes(r, half):
        meta_t = jnp.transpose(m2[r, pl.ds(half * 256, 256), :].astype(F32))
        ids_t, hi_t, lo_t = (meta_t[i * TOP:i * TOP + TOP] for i in range(3))
        sub = lax.broadcasted_iota(jnp.int32, (8, 256), 0)
        block = (lax.broadcasted_iota(jnp.int32, (8, 256), 1) // 32).astype(F32)
        present = jnp.zeros((8, 256), F32)
        terms = []
        c_axis = ORDERS[r][2]
        for c in range(4):
            expert = (dev + (c - at[c_axis]) * STRIDE[c_axis]).astype(F32)
            hit = ids_t == expert
            present = jnp.where(sub == c, jnp.sum(jnp.where(hit, 1.0, 0.0), axis=0, keepdims=True), present)
            terms.append([jnp.sum(jnp.where(hit, t, 0.0), axis=0, keepdims=True) for t in (hi_t, lo_t)])
        slot = jnp.dot(present.astype(BF16), upper, preferred_element_type=F32)
        return jnp.where(present > 0.5, block * 8.0 + slot, -1.0), terms

    def build_pick(r):
        for half in range(2):
            spot, _ = routes(r, half)
            for c in range(4):
                pick[r, half, pl.ds(c * 64, 64), :] = jnp.where(index == spot[c:c + 1], 1.0, 0.0).astype(BF16)

    def build_mix(r):
        for half in range(2):
            spot, terms = routes(r, half)
            for i in range(2):
                table = jnp.concatenate([jnp.where(index == spot[c:c + 1], terms[c][i], 0.0) for c in range(4)], axis=0)
                mix[r, half, i] = jnp.transpose(table).astype(BF16)

    def stage_c(q):
        r, j = UNITS[q]
        c_at = at[ORDERS[r][2]]
        far, _ = peer(ORDERS[r][1], 2)
        lanes = unit_lanes(q)
        if j == 0:
            wait_bytes(m2.at[r, pl.ds(0, 384), :], recv_m2.at[r])
            build_pick(r)
        wait_bytes(g2.at[aligned(far, 128), lanes], recv_far.at[q])
        wait_bytes(g2.at[aligned(far, 128), lanes], send_far.at[q])
        for half in range(2):
            v = jnp.dot(pick[r, half], g2[pl.ds(half * 256, 256), lanes], preferred_element_type=F32).astype(BF16)
            for c in range(4):
                sel[pl.ds(c * 128 + half * 64, 64), lanes] = v[c * 64:c * 64 + 64]
        for shift in (1, 2, 3):
            other, target = peer(ORDERS[r][2], shift)
            send(sel.at[aligned(other, 128), lanes], xs.at[aligned(c_at, 128), lanes], send3, recv3.at[q], target)
        xs[aligned(c_at, 128), lanes] = sel[aligned(c_at, 128), lanes]

    def features(i):
        r, k0, kw, units = GROUPS[i]
        rows = pl.ds(k0, kw)
        for q in units:
            wait_bytes(xs.at[pl.ds(0, 384), unit_lanes(q)], recv3.at[q])
        wait_bytes(w1.at[rows, pl.ds(0, 2 * HALF)], w_local.at[i])
        wait_bytes(w1.at[rows, pl.ds(0, 2 * HALF)], w_recv.at[i])
        where = tile_map(r)

        if i < len(GROUPS) - 1:
            def step(n, carry, r=r, rows=rows, first=(i == 0), where=where):
                cols = pl.ds(pl.multiple_of(n * CHUNK, CHUNK), CHUNK)
                res = jnp.dot(xs[:, rows], w1[rows, cols], preferred_element_type=F32)
                if first:
                    acc[:, cols] = res
                elif r == 0:
                    acc[:, cols] += res
                else:
                    for p in range(64):
                        acc[pl.ds(where[p] * 8, 8), cols] += res[p * 8:p * 8 + 8]
                return carry

            lax.fori_loop(0, 4 * HALF // CHUNK, step, 0)
        else:
            def last(n, carry, rows=rows):
                at_gate = pl.ds(pl.multiple_of(n * LAST, LAST), LAST)
                at_up = pl.ds(pl.multiple_of(2 * HALF + n * LAST, LAST), LAST)
                v = acc[:, at_gate] + jnp.dot(xs[:, rows], w1[rows, at_gate], preferred_element_type=F32)
                u = acc[:, at_up] + jnp.dot(xs[:, rows], w1[rows, at_up], preferred_element_type=F32)
                act[:, at_gate] = (v / (1.0 + jnp.exp(-v)) * u).astype(BF16)
                return carry

            lax.fori_loop(0, 2 * HALF // LAST, last, 0)
        if i == FREED:
            wait_bytes(down_other, d_recv)
            for q in range(EARLY):
                pltpu.make_async_copy(down_other.at[:, unit_lanes(q)],
                                      wd.at[pl.ds(HALF, HALF), pl.ds(q * WIDTH, WIDTH)], d_local.at[q]).start()
            for r in (1, 2, 0):
                theirs, cols = pl.ds(BLOCK_AT[r], BLOCK), pl.ds(r * BLOCK, BLOCK)
                sem = d_local.at[EARLY + r]
                pltpu.make_async_copy(w_down.at[:, theirs], w1.at[pl.ds(LATER, HALF), cols], sem).start()
                pltpu.make_async_copy(down_other.at[:, theirs], w1.at[pl.ds(LATER + HALF, HALF), cols], sem).start()

    for q in range(NU):
        stage_c(q)
        for i, after in enumerate(BETWEEN):
            if q == after:
                features(i)
    for r in range(3):
        build_mix(r)
    for i in range(len(BETWEEN), len(GROUPS)):
        features(i)

    wait_bytes(sel.at[pl.ds(0, 384), :], send3)
    wait_bytes(g1.at[pl.ds(0, 96), :], send1)
    wait_bytes(g2.at[pl.ds(0, 256), :], send2)

    def down_c(q):
        r, j = UNITS[q]
        c_at = at[ORDERS[r][2]]
        lanes = unit_lanes(q)
        if q < EARLY:
            down = wd.at[:, pl.ds(q * WIDTH, WIDTH)]
            wait_bytes(down, d_local.at[q])
        else:
            block = w1.at[pl.ds(LATER, 2 * HALF), pl.ds(r * BLOCK, BLOCK)]
            start = BASE[r] + j * WIDTH - BLOCK_AT[r]
            down = block.at[:, pl.ds(start, WIDTH)]
            if start == 0:
                wait_bytes(block, d_local.at[EARLY + r])
        res = jnp.dot(act[...], down[...], preferred_element_type=F32)
        where = tile_map(r)
        for p in range(0, 64, 2):
            pair = jnp.concatenate([res[where[p + i] * 8:where[p + i] * 8 + 8] for i in range(2)], axis=0)
            sel[pl.ds(p * 8, 16), lanes] = pair.astype(BF16)
        for shift in (1, 2, 3):
            other, target = peer(ORDERS[r][2], shift)
            send(sel.at[aligned(other, 128), lanes], g2.at[aligned(c_at, 128), lanes], send_c, recv_c.at[q], target)
        g2[aligned(c_at, 128), lanes] = sel[aligned(c_at, 128), lanes]

    def combine(q):
        r, _ = UNITS[q]
        axis = ORDERS[r][1]
        lanes = unit_lanes(q)
        wait_bytes(g2.at[pl.ds(0, 384), lanes], recv_c.at[q])
        for half in range(2):
            v = jnp.concatenate([g2[pl.ds(m * 128 + half * 64, 64), lanes] for m in range(4)], axis=0)
            total = jnp.dot(mix[r, half, 0], v, preferred_element_type=F32)
            total += jnp.dot(mix[r, half, 1], v, preferred_element_type=F32)
            xs[pl.ds(half * 256, 256), lanes] = total.astype(BF16)
        far, _ = peer(axis, 2)
        for i, shift in enumerate((1, 3)):
            _, target = peer(axis, shift)
            view = half_lanes(q, i)
            send(xs.at[aligned(far, 128), view], rt.at[:, view], send_t, recv_t.at[q], target)

    def join(q):
        axis = ORDERS[UNITS[q][0]][1]
        lanes = unit_lanes(q)
        wait_bytes(rt.at[:, lanes], recv_t.at[q])
        for i, shift in enumerate((1, 3)):
            other, target = peer(axis, shift)
            rows, view = aligned(other, 128), half_lanes(q, i)
            xs[rows, view] = (xs[rows, view].astype(F32) + rt[:, view].astype(F32)).astype(BF16)
            send(xs.at[rows, lanes], rb.at[pl.ds(i * 128, 128), lanes], send_b, recv_b.at[q], target)

    def sum_b(q):
        r, _ = UNITS[q]
        a = at[ORDERS[r][0]]
        lanes = unit_lanes(q)
        wait_bytes(rb.at[:, lanes], recv_b.at[q])
        total = xs[aligned(at[ORDERS[r][1]], 128), lanes].astype(F32)
        for m in range(2):
            total += rb[pl.ds(m * 128, 128), lanes].astype(F32)
        g1[:, lanes] = total.astype(BF16)
        for shift in (1, 2, 3):
            other, target = peer(ORDERS[r][0], shift)
            send(g1.at[aligned(other, 32), lanes], ra.at[aligned(a, 32), lanes], send_a, recv_a.at[q], target)
        ra[aligned(a, 32), lanes] = g1[aligned(a, 32), lanes]

    def finish(q):
        lanes = unit_lanes(q)
        wait_bytes(ra.at[pl.ds(0, 96), lanes], recv_a.at[q])
        total = ra[pl.ds(0, 32), lanes].astype(F32)
        for m in range(1, 4):
            total += ra[pl.ds(m * 32, 32), lanes].astype(F32)
        out[:, lanes] = (hidden[:, lanes].astype(F32) + total).astype(BF16)

    for t in range(NU + BACK[-1]):
        for step, late in zip((down_c, combine, join, sum_b, finish), BACK):
            if 0 <= t - late < NU:
                apart(step, t - late)

    wait_bytes(m1.at[:, pl.ds(0, 96), :], send_m)
    wait_bytes(m2.at[:, pl.ds(0, 384), :], send_m)
    wait_bytes(w1.at[:, pl.ds(0, 2 * HALF)], w_send)
    wait_bytes(down_other, w_send)
    wait_bytes(sel.at[pl.ds(0, 384), :], send_c)
    wait_bytes(rt, send_t)
    wait_bytes(rb, send_b)
    wait_bytes(g1.at[pl.ds(0, 96), :], send_a)


def local(hidden, norm_gain, expert_ids, gate_values, w_gate, w_up, w_down):
    vmem = pl.BlockSpec(memory_space=pltpu.VMEM)
    anywhere = pl.BlockSpec(memory_space=pl.ANY)
    dma = pltpu.SemaphoreType.DMA
    buf = pltpu.VMEM
    out, _ = pl.pallas_call(
        body,
        out_shape=(
            jax.ShapeDtypeStruct((ROWS, D), BF16),
            jax.ShapeDtypeStruct((HALF, D), BF16),
        ),
        in_specs=[vmem] * 4 + [anywhere] * 3,
        out_specs=(vmem, anywhere),
        scratch_shapes=[
            buf((128, D), BF16), buf((512, D), BF16), buf((512, D), BF16), buf((512, D), BF16),
            buf((128, D), BF16), buf((256, D), BF16), buf((128, D), BF16),
            buf((512, 4 * HALF), F32), buf((512, 2 * HALF), BF16),
            buf((D, 4 * HALF), BF16), buf((2 * HALF, EARLY * WIDTH), BF16),
            buf((3, 128, 128), BF16), buf((3, 512, 128), BF16),
            buf((3, 2, 256, 256), BF16), buf((3, 2, 2, 256, 256), BF16),
        ] + [dma((NU,))] * 10 + [dma((3,))] * 2 + [dma] * 8 + [
            dma((len(GROUPS),)), dma((len(GROUPS),)), dma, dma, dma((EARLY + 3,)),
        ],
        compiler_params=pltpu.CompilerParams(
            collective_id=0, has_side_effects=True, vmem_limit_bytes=60 * 2**20
        ),
        name="expert_layer",
    )(hidden, norm_gain.reshape(D // 128, 128), expert_ids.T, gate_values.T, w_gate[0], w_up[0], w_down[0])
    return out


def solution(mesh):
    return jax.shard_map(
        local,
        mesh=mesh,
        in_specs=(
            P(("grp", "dev"), None),
            P(),
            P(("grp", "dev"), None),
            P(("grp", "dev"), None),
            P("dev", None, "grp"),
            P("dev", None, "grp"),
            P("dev", "grp", None),
        ),
        out_specs=P(("grp", "dev"), None),
        check_vma=False,
    )
```

```python
import functools

import jax
import jax.numpy as jnp
from jax import lax
from jax.experimental import pallas as pl
from jax.experimental.pallas import tpu as pltpu
from jax.sharding import PartitionSpec as P

D = 4096
HALF = 768
TOP = 8
ROWS = 32
EPS = 1e-06
MESH = pl.DeviceIdType.MESH
F32, BF16 = jnp.float32, jnp.bfloat16

ORDERS = (("y", "z", "x"), ("z", "x", "y"), ("x", "y", "z"))
STRIDE = {"y": 16, "z": 4, "x": 1}
COUNT = (6, 5, 5)
BASE = (0, 1536, 2816)
WIDTH = 256
UNITS = [(r, j) for j in range(6) for r in range(3) if j < COUNT[r]]
NU = len(UNITS)
GROUPS = []
for _i, _order in enumerate(((0, 1, 2), (0, 1, 2), (1, 2, 0))):
    for _r in _order:
        _js = [j for j in (2 * _i, 2 * _i + 1) if j < COUNT[_r]]
        GROUPS.append((_r, BASE[_r] + _js[0] * WIDTH, len(_js) * WIDTH, [UNITS.index((_r, j)) for j in _js]))
FREED = max(i for i, grp in enumerate(GROUPS) if grp[0] == 1)
LATER = BASE[1]
EARLY = 4
BLOCK = 1024
BLOCK_AT = [BASE[r] + UNITS[:EARLY].count((r, 0)) * WIDTH + UNITS[:EARLY].count((r, 1)) * WIDTH for r in range(3)]
LAG = 16
BETWEEN = ()
BACK = (0, 16, 32, 48, 64)
CHUNK = 1536
LAST = 512


def tile_map(r):
    out = []
    for p in range(64):
        at = dict(zip(ORDERS[r], (p % 4, p // 4 % 4, p // 16)))
        out.append(at[ORDERS[0][2]] * 16 + at[ORDERS[0][1]] * 4 + at[ORDERS[0][0]])
    return out


def unit_lanes(q):
    r, j = UNITS[q]
    return pl.ds(BASE[r] + j * WIDTH, WIDTH)


def half_lanes(q, i):
    r, j = UNITS[q]
    return pl.ds(BASE[r] + j * WIDTH + i * (WIDTH // 2), WIDTH // 2)


def aligned(index, rows):
    return pl.ds(pl.multiple_of(index * rows, rows), rows)


def wait_bytes(view, sem):
    pltpu.make_async_copy(view, view, sem).wait()


def body(hidden, gain, ids, gates, w_gate, w_up, w_down, out, down_other,
         g1, g2, sel, xs, rt, rb, ra, acc, act, w1, wd, m1, m2, pick, mix,
         recv1, recv_up, recv_dn, recv_far, recv3, recv_c, recv_t, recv_b, recv_a, send_far,
         recv_m1, recv_m2, send1, send2, send3, send_c, send_t, send_b, send_a, send_m,
         w_local, w_recv, w_send, d_recv, d_local):
    grp = lax.axis_index("grp")
    dev = lax.axis_index("dev")
    at = {"y": dev // 16, "z": (dev // 4) % 4, "x": dev % 4}

    def apart(step, q):
        def once(_, carry):
            step(q)
            return carry

        lax.fori_loop(0, 1 + dev // 64, once, 0)

    def peer(axis, shift):
        other = (at[axis] + shift) % 4
        return other, dev + (other - at[axis]) * STRIDE[axis]

    def send(src, dst, ssem, rsem, target):
        pltpu.make_async_remote_copy(
            src_ref=src, dst_ref=dst, send_sem=ssem, recv_sem=rsem,
            device_id=(grp, target), device_id_type=MESH,
        ).start()

    barrier = pltpu.get_barrier_semaphore()
    for axis in ("y", "z", "x"):
        for shift in (1, 2, 3):
            _, target = peer(axis, shift)
            pl.semaphore_signal(barrier, inc=1, device_id=(grp, target), device_id_type=MESH)
    pl.semaphore_signal(barrier, inc=1, device_id=(1 - grp, dev), device_id_type=MESH)

    for i, (r, k0, kw, _) in enumerate(GROUPS):
        rows = pl.ds(k0, kw)
        pltpu.make_async_copy(w_gate.at[rows], w1.at[rows, pl.ds(0, HALF)], w_local.at[i]).start()
        pltpu.make_async_copy(w_up.at[rows], w1.at[rows, pl.ds(2 * HALF, HALF)], w_local.at[i]).start()
    for q in range(EARLY):
        pltpu.make_async_copy(w_down.at[:, unit_lanes(q)], wd.at[pl.ds(0, HALF), pl.ds(q * WIDTH, WIDTH)],
                              d_local.at[q]).start()

    squares = jnp.zeros((ROWS, WIDTH), F32)
    for q in range(NU):
        part = hidden[:, unit_lanes(q)].astype(F32)
        squares += part * part
    factor = lax.rsqrt(jnp.sum(squares, axis=1, keepdims=True) * (1.0 / D) + EPS)
    for q, (r, _) in enumerate(UNITS):
        lanes = unit_lanes(q)
        row = (BASE[r] + UNITS[q][1] * WIDTH) // 128
        scale = jnp.concatenate([gain[row + i:row + i + 1, :] for i in range(WIDTH // 128)], axis=1).astype(F32)
        part = hidden[:, lanes].astype(F32) * factor * scale
        g1[aligned(at[ORDERS[r][0]], 32), lanes] = part.astype(BF16)
    gate_v = gates[...]
    weight = gate_v / jnp.sum(gate_v, axis=0, keepdims=True)
    w_hi = weight.astype(BF16).astype(F32)
    routing = jnp.concatenate([ids[...].astype(F32), w_hi, weight - w_hi, jnp.zeros((TOP, ROWS), F32)], axis=0)
    eye = jnp.where(lax.broadcasted_iota(jnp.int32, (4 * TOP, 128), 0) == lax.broadcasted_iota(jnp.int32, (4 * TOP, 128), 1),
                    1.0, 0.0).astype(BF16)
    meta = lax.dot_general(routing.astype(BF16), eye, (((0,), (0,)), ((), ())), preferred_element_type=F32).astype(BF16)
    for r in range(3):
        a = at[ORDERS[r][0]]
        m1[r, aligned(a, 32), :] = meta

    pl.semaphore_wait(barrier, 10)

    for r in range(3):
        a = at[ORDERS[r][0]]
        for shift in (1, 2, 3):
            _, target = peer(ORDERS[r][0], shift)
            view = m1.at[r, aligned(a, 32), :]
            send(view, view, send_m, recv_m1.at[r], target)
    for q, (r, _) in enumerate(UNITS):
        a = at[ORDERS[r][0]]
        for shift in (1, 2, 3):
            _, target = peer(ORDERS[r][0], shift)
            view = g1.at[aligned(a, 32), unit_lanes(q)]
            send(view, view, send1, recv1.at[q], target)

    def send_other(src, dst, rsem):
        pltpu.make_async_remote_copy(
            src_ref=src, dst_ref=dst, send_sem=w_send, recv_sem=rsem,
            device_id=(1 - grp, dev), device_id_type=MESH,
        ).start()

    def send_weights(i):
        if i < len(GROUPS):
            rows = pl.ds(GROUPS[i][1], GROUPS[i][2])
            send_other(w_gate.at[rows], w1.at[rows, pl.ds(HALF, HALF)], w_recv.at[i])
            send_other(w_up.at[rows], w1.at[rows, pl.ds(3 * HALF, HALF)], w_recv.at[i])
        elif i == len(GROUPS):
            send_other(w_down, down_other, d_recv)

    def stage_b(q):
        r, j = UNITS[q]
        axis = ORDERS[r][1]
        b = at[axis]
        lanes = unit_lanes(q)
        wait_bytes(g1.at[pl.ds(0, 96), lanes], recv1.at[q])
        for shift, sem in ((1, recv_up), (3, recv_dn)):
            _, target = peer(axis, shift)
            send(g1.at[:, lanes], g2.at[aligned(b, 128), lanes], send2, sem.at[q], target)
        g2[aligned(b, 128), lanes] = g1[:, lanes]
        if j == 0:
            wait_bytes(m1.at[r, pl.ds(0, 96), :], recv_m1.at[r])
            for shift in (1, 2, 3):
                _, target = peer(axis, shift)
                send(m1.at[r], m2.at[r, aligned(b, 128), :], send_m, recv_m2.at[r], target)
            m2[r, aligned(b, 128), :] = m1[r]
        send_weights(q)

    def pass_on(q):
        axis = ORDERS[UNITS[q][0]][1]
        for i, (shift, sem) in enumerate(((1, recv_up), (3, recv_dn))):
            came, _ = peer(axis, 4 - shift)
            _, target = peer(axis, shift)
            wait_bytes(g2.at[aligned(came, 128), unit_lanes(q)], sem.at[q])
            view = g2.at[aligned(came, 128), half_lanes(q, i)]
            send(view, view, send_far.at[q], recv_far.at[q], target)

    for t in range(NU + LAG):
        if t < NU:
            stage_b(t)
        if t >= LAG:
            pass_on(t - LAG)

    row_s = lax.broadcasted_iota(jnp.int32, (256, 256), 0)
    col_s = lax.broadcasted_iota(jnp.int32, (256, 256), 1)
    upper = jnp.where((row_s // 32 == col_s // 32) & (row_s < col_s), 1.0, 0.0).astype(BF16)
    index = lax.broadcasted_iota(jnp.int32, (64, 256), 0).astype(F32)

    def routes(r, half):
        meta_t = jnp.transpose(m2[r, pl.ds(half * 256, 256), :].astype(F32))
        ids_t, hi_t, lo_t = (meta_t[i * TOP:i * TOP + TOP] for i in range(3))
        sub = lax.broadcasted_iota(jnp.int32, (8, 256), 0)
        block = (lax.broadcasted_iota(jnp.int32, (8, 256), 1) // 32).astype(F32)
        present = jnp.zeros((8, 256), F32)
        terms = []
        c_axis = ORDERS[r][2]
        for c in range(4):
            expert = (dev + (c - at[c_axis]) * STRIDE[c_axis]).astype(F32)
            hit = ids_t == expert
            present = jnp.where(sub == c, jnp.sum(jnp.where(hit, 1.0, 0.0), axis=0, keepdims=True), present)
            terms.append([jnp.sum(jnp.where(hit, t, 0.0), axis=0, keepdims=True) for t in (hi_t, lo_t)])
        slot = jnp.dot(present.astype(BF16), upper, preferred_element_type=F32)
        return jnp.where(present > 0.5, block * 8.0 + slot, -1.0), terms

    def build_pick(r):
        for half in range(2):
            spot, _ = routes(r, half)
            for c in range(4):
                pick[r, half, pl.ds(c * 64, 64), :] = jnp.where(index == spot[c:c + 1], 1.0, 0.0).astype(BF16)

    def build_mix(r):
        for half in range(2):
            spot, terms = routes(r, half)
            for i in range(2):
                table = jnp.concatenate([jnp.where(index == spot[c:c + 1], terms[c][i], 0.0) for c in range(4)], axis=0)
                mix[r, half, i] = jnp.transpose(table).astype(BF16)

    def stage_c(q):
        r, j = UNITS[q]
        c_at = at[ORDERS[r][2]]
        far, _ = peer(ORDERS[r][1], 2)
        lanes = unit_lanes(q)
        if j == 0:
            wait_bytes(m2.at[r, pl.ds(0, 384), :], recv_m2.at[r])
            build_pick(r)
        wait_bytes(g2.at[aligned(far, 128), lanes], recv_far.at[q])
        wait_bytes(g2.at[aligned(far, 128), lanes], send_far.at[q])
        for half in range(2):
            v = jnp.dot(pick[r, half], g2[pl.ds(half * 256, 256), lanes], preferred_element_type=F32).astype(BF16)
            for c in range(4):
                sel[pl.ds(c * 128 + half * 64, 64), lanes] = v[c * 64:c * 64 + 64]
        for shift in (1, 2, 3):
            other, target = peer(ORDERS[r][2], shift)
            send(sel.at[aligned(other, 128), lanes], xs.at[aligned(c_at, 128), lanes], send3, recv3.at[q], target)
        xs[aligned(c_at, 128), lanes] = sel[aligned(c_at, 128), lanes]

    def features(i):
        r, k0, kw, units = GROUPS[i]
        rows = pl.ds(k0, kw)
        for q in units:
            wait_bytes(xs.at[pl.ds(0, 384), unit_lanes(q)], recv3.at[q])
        wait_bytes(w1.at[rows, pl.ds(0, 2 * HALF)], w_local.at[i])
        wait_bytes(w1.at[rows, pl.ds(0, 2 * HALF)], w_recv.at[i])
        where = tile_map(r)

        if i < len(GROUPS) - 1:
            def step(n, carry, r=r, rows=rows, first=(i == 0), where=where):
                cols = pl.ds(pl.multiple_of(n * CHUNK, CHUNK), CHUNK)
                res = jnp.dot(xs[:, rows], w1[rows, cols], preferred_element_type=F32)
                if first:
                    acc[:, cols] = res
                elif r == 0:
                    acc[:, cols] += res
                else:
                    for p in range(64):
                        acc[pl.ds(where[p] * 8, 8), cols] += res[p * 8:p * 8 + 8]
                return carry

            lax.fori_loop(0, 4 * HALF // CHUNK, step, 0)
        else:
            def last(n, carry, rows=rows):
                at_gate = pl.ds(pl.multiple_of(n * LAST, LAST), LAST)
                at_up = pl.ds(pl.multiple_of(2 * HALF + n * LAST, LAST), LAST)
                v = acc[:, at_gate] + jnp.dot(xs[:, rows], w1[rows, at_gate], preferred_element_type=F32)
                u = acc[:, at_up] + jnp.dot(xs[:, rows], w1[rows, at_up], preferred_element_type=F32)
                act[:, at_gate] = (v / (1.0 + jnp.exp(-v)) * u).astype(BF16)
                return carry

            lax.fori_loop(0, 2 * HALF // LAST, last, 0)
        if i == FREED:
            wait_bytes(down_other, d_recv)
            for q in range(EARLY):
                pltpu.make_async_copy(down_other.at[:, unit_lanes(q)],
                                      wd.at[pl.ds(HALF, HALF), pl.ds(q * WIDTH, WIDTH)], d_local.at[q]).start()
            for r in (1, 2, 0):
                theirs, cols = pl.ds(BLOCK_AT[r], BLOCK), pl.ds(r * BLOCK, BLOCK)
                sem = d_local.at[EARLY + r]
                pltpu.make_async_copy(w_down.at[:, theirs], w1.at[pl.ds(LATER, HALF), cols], sem).start()
                pltpu.make_async_copy(down_other.at[:, theirs], w1.at[pl.ds(LATER + HALF, HALF), cols], sem).start()

    for q in range(NU):
        stage_c(q)
        for i, after in enumerate(BETWEEN):
            if q == after:
                features(i)
    for r in range(3):
        build_mix(r)
    for i in range(len(BETWEEN), len(GROUPS)):
        features(i)

    wait_bytes(sel.at[pl.ds(0, 384), :], send3)
    wait_bytes(g1.at[pl.ds(0, 96), :], send1)
    wait_bytes(g2.at[pl.ds(0, 256), :], send2)

    def down_c(q):
        r, j = UNITS[q]
        c_at = at[ORDERS[r][2]]
        lanes = unit_lanes(q)
        if q < EARLY:
            down = wd.at[:, pl.ds(q * WIDTH, WIDTH)]
            wait_bytes(down, d_local.at[q])
        else:
            block = w1.at[pl.ds(LATER, 2 * HALF), pl.ds(r * BLOCK, BLOCK)]
            start = BASE[r] + j * WIDTH - BLOCK_AT[r]
            down = block.at[:, pl.ds(start, WIDTH)]
            if start == 0:
                wait_bytes(block, d_local.at[EARLY + r])
        res = jnp.dot(act[...], down[...], preferred_element_type=F32)
        where = tile_map(r)
        for p in range(0, 64, 2):
            pair = jnp.concatenate([res[where[p + i] * 8:where[p + i] * 8 + 8] for i in range(2)], axis=0)
            sel[pl.ds(p * 8, 16), lanes] = pair.astype(BF16)
        for shift in (1, 2, 3):
            other, target = peer(ORDERS[r][2], shift)
            send(sel.at[aligned(other, 128), lanes], g2.at[aligned(c_at, 128), lanes], send_c, recv_c.at[q], target)
        g2[aligned(c_at, 128), lanes] = sel[aligned(c_at, 128), lanes]

    def combine(q):
        r, _ = UNITS[q]
        axis = ORDERS[r][1]
        lanes = unit_lanes(q)
        wait_bytes(g2.at[pl.ds(0, 384), lanes], recv_c.at[q])
        for half in range(2):
            v = jnp.concatenate([g2[pl.ds(m * 128 + half * 64, 64), lanes] for m in range(4)], axis=0)
            total = jnp.dot(mix[r, half, 0], v, preferred_element_type=F32)
            total += jnp.dot(mix[r, half, 1], v, preferred_element_type=F32)
            xs[pl.ds(half * 256, 256), lanes] = total.astype(BF16)
        far, _ = peer(axis, 2)
        for i, shift in enumerate((1, 3)):
            _, target = peer(axis, shift)
            view = half_lanes(q, i)
            send(xs.at[aligned(far, 128), view], rt.at[:, view], send_t, recv_t.at[q], target)

    def join(q):
        axis = ORDERS[UNITS[q][0]][1]
        lanes = unit_lanes(q)
        wait_bytes(rt.at[:, lanes], recv_t.at[q])
        for i, shift in enumerate((1, 3)):
            other, target = peer(axis, shift)
            rows, view = aligned(other, 128), half_lanes(q, i)
            xs[rows, view] = (xs[rows, view].astype(F32) + rt[:, view].astype(F32)).astype(BF16)
            send(xs.at[rows, lanes], rb.at[pl.ds(i * 128, 128), lanes], send_b, recv_b.at[q], target)

    def sum_b(q):
        r, _ = UNITS[q]
        a = at[ORDERS[r][0]]
        lanes = unit_lanes(q)
        wait_bytes(rb.at[:, lanes], recv_b.at[q])
        total = xs[aligned(at[ORDERS[r][1]], 128), lanes].astype(F32)
        for m in range(2):
            total += rb[pl.ds(m * 128, 128), lanes].astype(F32)
        g1[:, lanes] = total.astype(BF16)
        for shift in (1, 2, 3):
            other, target = peer(ORDERS[r][0], shift)
            send(g1.at[aligned(other, 32), lanes], ra.at[aligned(a, 32), lanes], send_a, recv_a.at[q], target)
        ra[aligned(a, 32), lanes] = g1[aligned(a, 32), lanes]

    def finish(q):
        lanes = unit_lanes(q)
        wait_bytes(ra.at[pl.ds(0, 96), lanes], recv_a.at[q])
        total = ra[pl.ds(0, 32), lanes].astype(F32)
        for m in range(1, 4):
            total += ra[pl.ds(m * 32, 32), lanes].astype(F32)
        out[:, lanes] = (hidden[:, lanes].astype(F32) + total).astype(BF16)

    for t in range(NU + BACK[-1]):
        for step, late in zip((down_c, combine, join, sum_b, finish), BACK):
            if 0 <= t - late < NU:
                apart(step, t - late)

    wait_bytes(m1.at[:, pl.ds(0, 96), :], send_m)
    wait_bytes(m2.at[:, pl.ds(0, 384), :], send_m)
    wait_bytes(w1.at[:, pl.ds(0, 2 * HALF)], w_send)
    wait_bytes(down_other, w_send)
    wait_bytes(sel.at[pl.ds(0, 384), :], send_c)
    wait_bytes(rt, send_t)
    wait_bytes(rb, send_b)
    wait_bytes(g1.at[pl.ds(0, 96), :], send_a)


def local(hidden, norm_gain, expert_ids, gate_values, w_gate, w_up, w_down):
    vmem = pl.BlockSpec(memory_space=pltpu.VMEM)
    anywhere = pl.BlockSpec(memory_space=pl.ANY)
    dma = pltpu.SemaphoreType.DMA
    buf = pltpu.VMEM
    out, _ = pl.pallas_call(
        body,
        out_shape=(
            jax.ShapeDtypeStruct((ROWS, D), BF16),
            jax.ShapeDtypeStruct((HALF, D), BF16),
        ),
        in_specs=[vmem] * 4 + [anywhere] * 3,
        out_specs=(vmem, anywhere),
        scratch_shapes=[
            buf((128, D), BF16), buf((512, D), BF16), buf((512, D), BF16), buf((512, D), BF16),
            buf((128, D), BF16), buf((256, D), BF16), buf((128, D), BF16),
            buf((512, 4 * HALF), F32), buf((512, 2 * HALF), BF16),
            buf((D, 4 * HALF), BF16), buf((2 * HALF, EARLY * WIDTH), BF16),
            buf((3, 128, 128), BF16), buf((3, 512, 128), BF16),
            buf((3, 2, 256, 256), BF16), buf((3, 2, 2, 256, 256), BF16),
        ] + [dma((NU,))] * 10 + [dma((3,))] * 2 + [dma] * 8 + [
            dma((len(GROUPS),)), dma((len(GROUPS),)), dma, dma, dma((EARLY + 3,)),
        ],
        compiler_params=pltpu.CompilerParams(
            collective_id=0, has_side_effects=True, vmem_limit_bytes=60 * 2**20
        ),
        name="expert_layer",
    )(hidden, norm_gain.reshape(D // 128, 128), expert_ids.T, gate_values.T, w_gate[0], w_up[0], w_down[0])
    return out


def solution(mesh):
    return jax.shard_map(
        local,
        mesh=mesh,
        in_specs=(
            P(("grp", "dev"), None),
            P(),
            P(("grp", "dev"), None),
            P(("grp", "dev"), None),
            P("dev", None, "grp"),
            P("dev", None, "grp"),
            P("dev", "grp", None),
        ),
        out_specs=P(("grp", "dev"), None),
        check_vma=False,
    )
```
